32 devices in a mesh: clip: 2 (over core), fsdp: 16 (over z, y, x).
Axes of the slice: x: 2, y: 2, z: 4, core: 2. Of those that a mesh axis runs over, the one named last changes fastest.
Arguments:
- span_queries: bfloat16 [16, 512, 2560], P('fsdp', None, 'clip'), may hold values from -20 to 20
- span_keys: bfloat16 [16, 512, 2560], P('fsdp', None, 'clip'), may hold values from -12 to 12
- span_values: bfloat16 [16, 512, 2560], P('fsdp', None, 'clip'), may hold values from -6 to 6
- cache_keys: bfloat16 [32, 512, 2560], P(None, 'fsdp', 'clip'), may hold values from -6 to 6
- cache_values: bfloat16 [32, 512, 2560], P(None, 'fsdp', 'clip'), may hold values from -6 to 6
- page_table: int32 [32], replicated, may hold values from 0 to 31, each once
- frame_lists: int32 [16, 6], replicated, may hold values from 0 to 15, as said below
- list_counts: int32 [16], replicated, may hold values from 1 to 6, as said below
- out_weight: bfloat16 [2560, 5120], P('clip', 'fsdp'), may hold values from -1 to 1
Outputs:
- projected: bfloat16 [16, 512, 5120], P('fsdp', 'clip')
The draws below stay inside these ranges and needn't reach their ends.
Inputs may be any that keep to these rules, and one draw needn't show every extreme that they name: `frame_lists`: each row holds 6 different cached frames; a frame attends to the first list_counts of them. `list_counts`: the counts of frames 2 * i and 2 * i + 1 sum to exactly 7; some frame attends to exactly 6. `page_table`: every block number once.
All inputs are finite; a program needn't handle non-finite values.
Results may differ from the reference program's by a relative error of at most 0.017.
Values may be sent and summed in bfloat16 or wider, within the bound.
A program may use at most 128 MiB of HBM per device.

```python
import math
import jax
import jax.numpy as jnp
from jax import lax

D = 5120
HD = 128
HEADS = 20
FT = 512
CF = 8
NC = 16
MAXL = 6
FRAMES = 16
BLOCKS = 32
N_CLIP = 2


def draw_together(key):
    pair_key = jax.random.fold_in(key, 101)
    subkeys = jax.random.split(pair_key, 2)
    array_shape = (FRAMES, FT, HEADS * HD)
    query_draw = 1.5 * jax.random.truncated_normal(subkeys[0], -4.0, 4.0, array_shape, jnp.float32)
    key_draw = jax.random.truncated_normal(subkeys[1], -4.0, 4.0, array_shape, jnp.float32)
    return (query_draw, key_draw)


def draw_span_queries(key, part):
    return draw_together(key)[0].astype(jnp.bfloat16)


def draw_span_keys(key, part):
    return draw_together(key)[1].astype(jnp.bfloat16)


def draw_frame_lists(key, part):
    list_key = jax.random.fold_in(key, 11)
    ranking_scores = jax.random.randint(list_key, (FRAMES, NC), 0, 1 << 20) * NC + jnp.arange(NC, dtype=jnp.int32)[None, :]
    ranking = jnp.argsort(ranking_scores, axis=1, stable=True).astype(jnp.int32)
    return ranking[:, :MAXL]


def draw_list_counts(key, part):
    subkeys = jax.random.split(jax.random.fold_in(key, 23), 2)
    pairs = FRAMES // 2
    first_counts = jax.random.randint(subkeys[0], (pairs,), 1, MAXL + 1)
    forced_pair = jax.random.randint(subkeys[1], (), 0, pairs)
    first_counts = jnp.where(jnp.arange(pairs, dtype=jnp.int32) == forced_pair, MAXL, first_counts)
    second_counts = MAXL + 1 - first_counts
    return jnp.stack([first_counts, second_counts], axis=1).reshape(FRAMES).astype(jnp.int32)


def steps_of(own_key, dims, cuts, low, high):
    loudness = 1.0
    for axis_at, shards_of in cuts:
        heights = jax.random.uniform(jax.random.fold_in(jax.random.fold_in(own_key, 6), axis_at), (shards_of,), jnp.float32, low / len(cuts), high / len(cuts))
        loudness = loudness * jnp.repeat(jnp.exp(heights), dims[axis_at] // shards_of).reshape((-1,) + (1,) * (len(dims) - 1 - axis_at))
    return loudness


def bell_draw(key, extent, width, most, cuts=(), kind=jnp.bfloat16):
    values = width * jax.random.normal(key, extent, jnp.float32)
    if cuts:
        values = values * steps_of(key, extent, cuts, -0.22, 0.18)
    return jnp.clip(values, -most, most).astype(kind)


def setup_inputs(seed: int = 0) -> dict:
    key_of = jax.random.split(jax.random.key(seed), 10)
    return {
        "span_queries": draw_span_queries(jax.random.fold_in(key_of[9], 71), 0),
        "span_keys": draw_span_keys(jax.random.fold_in(key_of[9], 71), 0),
        "span_values": bell_draw(key_of[2], (FRAMES, FT, HEADS * HD), 1.0, 6.0, ((0, 16), (2, 2))),
        "cache_keys": bell_draw(key_of[3], (BLOCKS, FT, HEADS * HD), 1.0, 6.0, ((1, 16), (2, 2))),
        "cache_values": bell_draw(key_of[4], (BLOCKS, FT, HEADS * HD), 1.0, 6.0, ((1, 16), (2, 2))),
        "page_table": jax.random.permutation(key_of[5], BLOCKS).astype(jnp.int32),
        "frame_lists": draw_frame_lists(jax.random.fold_in(key_of[9], 71), 0),
        "list_counts": draw_list_counts(jax.random.fold_in(key_of[9], 71), 0),
        "out_weight": bell_draw(key_of[8], (HEADS * HD, D), (HEADS * HD // 64) ** -0.5, 1.0, ((0, 2), (1, 16))),
    }


neg_fill = -1e+30

def one_frame(frame_item, cache_keys, cache_values, page_table, out_weight):
    query_rows, key_rows, value_rows, listed, item_count, frame_index = frame_item
    clip_index = frame_index // CF
    blocks = page_table[(clip_index * NC + listed).astype(jnp.int32)].astype(jnp.int32)
    key_set = jnp.concatenate([key_rows[None], cache_keys[blocks]], axis=0).reshape((MAXL + 1) * FT, HEADS, HD)
    value_set = jnp.concatenate([value_rows[None], cache_values[blocks]], axis=0).reshape((MAXL + 1) * FT, HEADS, HD)
    live_slots = jnp.arange(MAXL + 1, dtype=jnp.int32) <= item_count
    live_keys = jnp.repeat(live_slots, FT)
    scores = jnp.einsum('qhd,khd->qhk', query_rows.reshape(FT, HEADS, HD).astype(jnp.float32), key_set.astype(jnp.float32)) * (1.0 / math.sqrt(HD))
    scores = jnp.where(live_keys[None, None, :], scores, neg_fill)
    top_score = lax.optimization_barrier(jnp.max(scores, axis=2, keepdims=True))
    weights = jnp.exp(scores - top_score)
    denominators = lax.optimization_barrier(jnp.sum(weights, axis=2))
    rounded = lax.optimization_barrier(weights.astype(jnp.bfloat16)).astype(jnp.float32)
    summed = jnp.einsum('qhk,khd->qhd', rounded, value_set.astype(jnp.float32))
    attended = (summed / denominators[:, :, None]).reshape(FT, HEADS * HD).astype(jnp.bfloat16)
    group_width = HEADS // N_CLIP * HD
    combined = jnp.zeros((FT, D), jnp.float32)
    for group_index in range(N_CLIP):
        lower = group_index * group_width
        partial_value = jnp.dot(attended[:, lower:lower + group_width], out_weight[lower:lower + group_width], preferred_element_type=jnp.float32)
        combined = combined + lax.optimization_barrier(partial_value.astype(jnp.bfloat16)).astype(jnp.float32)
    return combined.astype(jnp.bfloat16)

def reference(span_queries, span_keys, span_values, cache_keys, cache_values, page_table, frame_lists, list_counts, out_weight):
    frame_numbers = jnp.arange(FRAMES, dtype=jnp.int32)

    def per_frame(frame_item):
        return one_frame(frame_item, cache_keys, cache_values, page_table, out_weight)
    return lax.map(per_frame, (span_queries, span_keys, span_values, frame_lists, list_counts, frame_numbers))
```

```python
import functools
import math

import jax
import jax.numpy as jnp
from jax import lax
from jax.experimental import pallas as pl
from jax.experimental.pallas import tpu as pltpu
from jax.sharding import PartitionSpec as P

HD = 128
CF = 8
NC = 16
FT = 512


neg_fill = -1e30


def lookup(values_table, positions):
    table_width = values_table.shape[0]
    matches = positions[..., None] == jnp.arange(table_width, dtype=jnp.int32)
    return jnp.sum(jnp.where(matches, values_table, 0), axis=-1)


def block_numbers(frame_index, slot_index, page_table, frame_lists):
    max_slots = frame_lists.shape[1]
    listed = lookup(frame_lists.reshape(-1), frame_index * max_slots + slot_index)
    return lookup(page_table, frame_index // CF * NC + listed)


def pick_blocks(send_blocks, cache_keys, cache_values):
    slot_total = send_blocks.shape[0]
    frames = send_blocks.shape[1]
    token_slice = cache_keys.shape[1]
    row_width = cache_keys.shape[2]
    sent_keys = cache_keys[send_blocks].reshape(slot_total, frames * token_slice, row_width)
    sent_values = cache_values[send_blocks].reshape(slot_total, frames * token_slice, row_width)
    return (sent_keys, sent_values)


def empty_state(tokens_here, heads_here):
    return (
        jnp.full((tokens_here, heads_here), neg_fill, jnp.float32),
        jnp.zeros((tokens_here, heads_here), jnp.float32),
        jnp.zeros((tokens_here, heads_here, HD), jnp.float32),
    )


def absorb(carried, query_block, key_block, value_block):
    running_max, running_sum, running_out = carried
    scores = jnp.einsum(
        "qhd,khd->qhk", query_block, key_block, preferred_element_type=jnp.float32
    ) * (1.0 / math.sqrt(HD))
    new_max = jnp.maximum(running_max, jnp.max(scores, axis=2))
    shrink = jnp.exp(running_max - new_max)
    weights = jnp.exp(scores - new_max[:, :, None])
    running_sum = running_sum * shrink + jnp.sum(weights, axis=2)
    running_out = running_out * shrink[:, :, None] + jnp.einsum(
        "qhk,khd->qhd",
        weights.astype(jnp.bfloat16),
        value_block,
        preferred_element_type=jnp.float32,
    )
    return (new_max, running_sum, running_out)


def local_general(
    span_queries,
    span_keys,
    span_values,
    cache_keys,
    cache_values,
    page_table,
    frame_lists,
    list_counts,
    out_weight,
):
    frames = lax.axis_size("fsdp")
    own_frame = lax.axis_index("fsdp")
    tokens_here = span_queries.shape[1]
    row_width = span_queries.shape[2]
    heads_here = row_width // HD
    max_slots = frame_lists.shape[1]
    own_queries = span_queries[0].reshape(tokens_here, heads_here, HD)
    own_keys = span_keys[0].reshape(tokens_here, heads_here, HD)
    own_values = span_values[0].reshape(tokens_here, heads_here, HD)
    destinations = jnp.arange(frames, dtype=jnp.int32)[:, None]
    blank = empty_state(tokens_here, heads_here)
    started = absorb(blank, own_queries, own_keys, own_values)
    slot_index = jnp.arange(max_slots, dtype=jnp.int32)[None, :]
    send_blocks = block_numbers(destinations, slot_index, page_table, frame_lists).T
    sent_keys, sent_values = pick_blocks(send_blocks, cache_keys, cache_values)
    arrived_keys, arrived_values = (
        lax.all_to_all(sent_keys, "fsdp", split_axis=1, concat_axis=1, tiled=True),
        lax.all_to_all(sent_values, "fsdp", split_axis=1, concat_axis=1, tiled=True),
    )
    arrived_keys = arrived_keys.reshape(max_slots, tokens_here, heads_here, HD)
    arrived_values = arrived_values.reshape(max_slots, tokens_here, heads_here, HD)
    item_count = lookup(list_counts, own_frame)

    def advance_own(item_number, carried_one):
        return absorb(
            carried_one, own_queries, arrived_keys[item_number], arrived_values[item_number]
        )

    final_state = lax.fori_loop(0, item_count, advance_own, started)
    running_sum = final_state[1]
    running_out = final_state[2]
    attended = (
        (running_out / running_sum[:, :, None]).astype(jnp.bfloat16).reshape(tokens_here, row_width)
    )
    partial_value = jnp.dot(
        attended,
        lax.all_gather(out_weight, "fsdp", axis=1, tiled=True),
        preferred_element_type=jnp.float32,
    )
    own_rows = lax.psum_scatter(
        partial_value.astype(jnp.bfloat16), "clip", scatter_dimension=0, tiled=True
    )
    return own_rows[None]


MESH = pl.DeviceIdType.MESH
LOG2E = 1.4426950408889634
VMEM_BYTES = 56 * 1024 * 1024


def attend_kernel(
    frames,
    slots,
    q_ref,
    k_ref,
    v_ref,
    ck_ref,
    cv_ref,
    page_ref,
    list_ref,
    count_ref,
    out_ref,
    send,
    recv,
    qkv,
    stage,
    att_in,
    o_s,
    m_s,
    l_s,
    blk,
    send_sem,
    recv_sem,
    qkv_sem,
    att_sem,
):
    me = lax.axis_index("fsdp")
    x_me = lax.rem(me, 2)
    partner = me + 1 - 2 * x_me
    heads = send.shape[0]
    half = heads * HD
    rows = q_ref.shape[0]
    scale = LOG2E / math.sqrt(HD)

    barrier = pltpu.get_barrier_semaphore()

    def greet(i, carry):
        pl.semaphore_signal(
            barrier, inc=1, device_id={"fsdp": lax.rem(me + i, frames)}, device_id_type=MESH
        )
        return carry

    lax.fori_loop(1, frames, greet, 0)
    pl.semaphore_wait(barrier, frames - 1)

    moves = []
    for t, ref in enumerate((q_ref, k_ref, v_ref)):
        theirs = pl.multiple_of((1 - x_me) * half, 128)
        mine = pl.multiple_of(x_me * half, 128)
        far = pltpu.make_async_remote_copy(
            src_ref=ref.at[:, pl.ds(theirs, half)],
            dst_ref=qkv.at[t, x_me],
            send_sem=qkv_sem.at[0, t],
            recv_sem=qkv_sem.at[1, t],
            device_id={"fsdp": partner},
            device_id_type=MESH,
        )
        near = pltpu.make_async_copy(
            ref.at[:, pl.ds(mine, half)], qkv.at[t, x_me], qkv_sem.at[2, t]
        )
        far.start()
        near.start()
        moves += [far, near]

    def number(p, carry):
        first = count_ref[2 * p]
        for j in range(slots):
            late = jnp.where(j >= first, 1, 0)
            at = jnp.minimum(j - late * first, slots - 2)
            listed = list_ref[2 * p + late, at]
            blk[p * slots + j] = page_ref[(2 * p) // CF * NC + listed]
        return carry

    lax.fori_loop(0, frames // 2, number, 0)

    def transfer(h, there, slot):
        return pltpu.make_async_remote_copy(
            src_ref=send.at[h, there],
            dst_ref=recv.at[h, slot],
            send_sem=send_sem.at[h, there],
            recv_sem=recv_sem.at[h, slot],
            device_id={"fsdp": there},
            device_id_type=MESH,
        )

    for h in range(heads):

        def fill(i, carry):
            there = lax.rem(me + i, frames)
            col = pl.multiple_of(lax.rem(there, 2) * half + h * HD, 128)
            base = there // 2 * slots
            for j in range(slots):
                b = blk[base + j]
                send[h, there, 0, j] = ck_ref[b, :, pl.ds(col, HD)]
                send[h, there, 1, j] = cv_ref[b, :, pl.ds(col, HD)]
            transfer(h, there, me).start()
            return carry

        lax.fori_loop(1, frames, fill, 0)
        col = pl.multiple_of(x_me * half + h * HD, 128)
        for j in range(slots):
            b = blk[me // 2 * slots + j]
            recv[h, me, 0, j] = ck_ref[b, :, pl.ds(col, HD)]
            recv[h, me, 1, j] = cv_ref[b, :, pl.ds(col, HD)]

    for move in moves:
        move.wait()

    first_me = count_ref[me - x_me]

    def attend(j, q, k, v):
        s = lax.dot_general(
            q, k, (((1,), (1,)), ((), ())), preferred_element_type=jnp.float32
        )
        top = jnp.max(s, axis=1, keepdims=True)
        w = jnp.exp2((s - top) * scale)
        m_s[j] = top
        l_s[j] = jnp.sum(w, axis=1, keepdims=True)
        o_s[j] = jnp.dot(w.astype(jnp.bfloat16), v, preferred_element_type=jnp.float32)

    att_moves = []
    for h in range(heads):
        cols = slice(h * HD, (h + 1) * HD)

        def own(f, carry):
            attend(slots + f, qkv[0, f, :, cols], qkv[1, f, :, cols], qkv[2, f, :, cols])
            return carry

        lax.fori_loop(0, 2, own, 0)

        def arrive(i, carry):
            there = lax.rem(me + i, frames)
            transfer(h, there, there).wait_recv()
            return carry

        lax.fori_loop(1, frames, arrive, 0)

        def listed(j, carry):
            f = jnp.where(j >= first_me, 1, 0)
            k = recv[h, :, 0, j].reshape(-1, HD)
            v = recv[h, :, 1, j].reshape(-1, HD)
            attend(j, qkv[0, f, :, cols], k, v)
            return carry

        lax.fori_loop(0, slots, listed, 0)

        for f in range(2):

            def live(j):
                if j >= slots:
                    return j - slots == f
                return (j < first_me) if f == 0 else (j >= first_me)

            tops = [
                m_s[j]
                if live(j) is True
                else jnp.where(live(j), m_s[j], jnp.float32(neg_fill))
                for j in range(slots + 2)
                if live(j) is not False
            ]
            top = functools.reduce(jnp.maximum, tops)
            total = jnp.zeros((rows, 1), jnp.float32)
            summed = jnp.zeros((rows, HD), jnp.float32)
            at = 0
            for j in range(slots + 2):
                if live(j) is False:
                    continue
                w = jnp.exp2((tops[at] - top) * scale)
                at += 1
                if live(j) is not True:
                    w = jnp.where(live(j), w, jnp.float32(0))
                total = total + w * l_s[j]
                summed = summed + w * o_s[j]
            stage[h, f] = (summed / total).astype(jnp.bfloat16)
        move = pltpu.make_async_remote_copy(
            src_ref=stage.at[h, 1 - x_me],
            dst_ref=att_in.at[h],
            send_sem=att_sem.at[0, h],
            recv_sem=att_sem.at[1, h],
            device_id={"fsdp": partner},
            device_id_type=MESH,
        )
        move.start()
        att_moves.append(move)
        out_ref[:, pl.ds(pl.multiple_of(x_me * half + h * HD, 128), HD)] = stage[h, x_me]

    for h in range(heads):
        att_moves[h].wait()
        out_ref[:, pl.ds(pl.multiple_of((1 - x_me) * half + h * HD, 128), HD)] = att_in[h]

    def drain(i, carry):
        there = lax.rem(me + i, frames)
        for h in range(heads):
            transfer(h, there, me).wait_send()
        return carry

    lax.fori_loop(1, frames, drain, 0)


def attend_pair(q, k, v, cache_keys, cache_values, page_table, frame_lists, list_counts, frames):
    rows, width = q.shape
    token_slice = cache_keys.shape[1]
    slots = frame_lists.shape[1] + 1
    heads = width // HD // 2
    block = (heads, frames, 2, slots, token_slice, HD)
    anywhere = pl.BlockSpec(memory_space=pl.ANY)
    vmem = pl.BlockSpec(memory_space=pltpu.VMEM)
    smem = pl.BlockSpec(memory_space=pltpu.SMEM)
    return pl.pallas_call(
        functools.partial(attend_kernel, frames, slots),
        out_shape=jax.ShapeDtypeStruct((rows, width), jnp.bfloat16),
        in_specs=[anywhere] * 3 + [vmem] * 2 + [smem] * 3,
        out_specs=vmem,
        scratch_shapes=[
            pltpu.VMEM(block, jnp.bfloat16),
            pltpu.VMEM(block, jnp.bfloat16),
            pltpu.VMEM((3, 2, rows, heads * HD), jnp.bfloat16),
            pltpu.VMEM((heads, 2, rows, HD), jnp.bfloat16),
            pltpu.VMEM((heads, rows, HD), jnp.bfloat16),
            pltpu.VMEM((slots + 2, rows, HD), jnp.float32),
            pltpu.VMEM((slots + 2, rows, 1), jnp.float32),
            pltpu.VMEM((slots + 2, rows, 1), jnp.float32),
            pltpu.SMEM((frames // 2 * slots,), jnp.int32),
            pltpu.SemaphoreType.DMA((heads, frames)),
            pltpu.SemaphoreType.DMA((heads, frames)),
            pltpu.SemaphoreType.DMA((3, 3)),
            pltpu.SemaphoreType.DMA((2, heads)),
        ],
        compiler_params=pltpu.CompilerParams(
            collective_id=0, has_side_effects=True, vmem_limit_bytes=VMEM_BYTES
        ),
        cost_estimate=pl.CostEstimate(
            flops=4 * rows * rows * HD * heads * (slots + 2),
            bytes_accessed=64 * 1024 * 1024,
            transcendentals=rows * rows * heads * (slots + 2),
        ),
    )(q, k, v, cache_keys, cache_values, page_table, frame_lists, list_counts)


def project_kernel(att_ref, w_ref, out_ref, sent, came, kept, send_sem, recv_sem):
    step = pl.program_id(0)
    steps, rows, wide = sent.shape
    me = lax.axis_index("clip")
    sibling = 1 - me

    @pl.when(step == 0)
    def _():
        barrier = pltpu.get_barrier_semaphore()
        pl.semaphore_signal(barrier, inc=1, device_id={"clip": sibling}, device_id_type=MESH)
        pl.semaphore_wait(barrier, 1)

    def move(i):
        return pltpu.make_async_remote_copy(
            src_ref=sent.at[i],
            dst_ref=came.at[i],
            send_sem=send_sem.at[i],
            recv_sem=recv_sem.at[i],
            device_id={"clip": sibling},
            device_id_type=MESH,
        )

    def product(half):
        start = pl.multiple_of(half * rows, rows)
        return lax.dot_general(
            att_ref[pl.ds(start, rows), :],
            w_ref[...],
            (((1,), (1,)), ((), ())),
            preferred_element_type=jnp.float32,
        ).astype(jnp.bfloat16)

    sent[step] = product(sibling)
    move(step).start()
    kept[step] = product(me)

    @pl.when(step == steps - 1)
    def _():
        for i in range(steps):
            move(i).wait()
            out_ref[:, i * wide : (i + 1) * wide] = (
                kept[i].astype(jnp.float32) + came[i].astype(jnp.float32)
            ).astype(jnp.bfloat16)


def project(attended, weights):
    columns, depth = weights.shape
    steps = 4
    wide = columns // steps
    rows = attended.shape[0] // 2
    block = (steps, rows, wide)
    return pl.pallas_call(
        project_kernel,
        grid=(steps,),
        out_shape=jax.ShapeDtypeStruct((rows, columns), jnp.bfloat16),
        in_specs=[
            pl.BlockSpec((2 * rows, depth), lambda i: (0, 0)),
            pl.BlockSpec((wide, depth), lambda i: (i, 0)),
        ],
        out_specs=pl.BlockSpec((rows, columns), lambda i: (0, 0)),
        scratch_shapes=[
            pltpu.VMEM(block, jnp.bfloat16),
            pltpu.VMEM(block, jnp.bfloat16),
            pltpu.VMEM(block, jnp.bfloat16),
            pltpu.SemaphoreType.DMA((steps,)),
            pltpu.SemaphoreType.DMA((steps,)),
        ],
        compiler_params=pltpu.CompilerParams(
            collective_id=1, has_side_effects=True, vmem_limit_bytes=VMEM_BYTES
        ),
    )(attended, weights)


def local(
    span_queries,
    span_keys,
    span_values,
    cache_keys,
    cache_values,
    page_table,
    frame_lists,
    list_counts,
    out_weight,
):
    frames = lax.axis_size("fsdp")
    attended = attend_pair(
        span_queries[0],
        span_keys[0],
        span_values[0],
        cache_keys,
        cache_values,
        page_table,
        frame_lists,
        list_counts,
        frames,
    )
    weights = lax.all_gather(out_weight.T, "fsdp", axis=0, tiled=True)
    return project(attended, weights)[None]


def solution(mesh):
    in_specs = (
        P("fsdp", None, "clip"),
        P("fsdp", None, "clip"),
        P("fsdp", None, "clip"),
        P(None, "fsdp", "clip"),
        P(None, "fsdp", "clip"),
        P(),
        P(),
        P(),
        P("clip", "fsdp"),
    )
    out_specs = P("fsdp", "clip", None)
    clip, fsdp = mesh.shape["clip"], mesh.shape["fsdp"]
    paired = clip == 2 and fsdp % 4 == 0 and FT // fsdp % 16 == 0
    body = local if paired else local_general
    return jax.shard_map(body, mesh=mesh, in_specs=in_specs, out_specs=out_specs, check_vma=False)
```

```python
import functools
import math

import jax
import jax.numpy as jnp
from jax import lax
from jax.experimental import pallas as pl
from jax.experimental.pallas import tpu as pltpu
from jax.sharding import PartitionSpec as P

HD = 128
CF = 8
NC = 16
FT = 512


neg_fill = -1e30


def lookup(values_table, positions):
    table_width = values_table.shape[0]
    matches = positions[..., None] == jnp.arange(table_width, dtype=jnp.int32)
    return jnp.sum(jnp.where(matches, values_table, 0), axis=-1)


def block_numbers(frame_index, slot_index, page_table, frame_lists):
    max_slots = frame_lists.shape[1]
    listed = lookup(frame_lists.reshape(-1), frame_index * max_slots + slot_index)
    return lookup(page_table, frame_index // CF * NC + listed)


def pick_blocks(send_blocks, cache_keys, cache_values):
    slot_total = send_blocks.shape[0]
    frames = send_blocks.shape[1]
    token_slice = cache_keys.shape[1]
    row_width = cache_keys.shape[2]
    sent_keys = cache_keys[send_blocks].reshape(slot_total, frames * token_slice, row_width)
    sent_values = cache_values[send_blocks].reshape(slot_total, frames * token_slice, row_width)
    return (sent_keys, sent_values)


def empty_state(tokens_here, heads_here):
    return (
        jnp.full((tokens_here, heads_here), neg_fill, jnp.float32),
        jnp.zeros((tokens_here, heads_here), jnp.float32),
        jnp.zeros((tokens_here, heads_here, HD), jnp.float32),
    )


def absorb(carried, query_block, key_block, value_block):
    running_max, running_sum, running_out = carried
    scores = jnp.einsum(
        "qhd,khd->qhk", query_block, key_block, preferred_element_type=jnp.float32
    ) * (1.0 / math.sqrt(HD))
    new_max = jnp.maximum(running_max, jnp.max(scores, axis=2))
    shrink = jnp.exp(running_max - new_max)
    weights = jnp.exp(scores - new_max[:, :, None])
    running_sum = running_sum * shrink + jnp.sum(weights, axis=2)
    running_out = running_out * shrink[:, :, None] + jnp.einsum(
        "qhk,khd->qhd",
        weights.astype(jnp.bfloat16),
        value_block,
        preferred_element_type=jnp.float32,
    )
    return (new_max, running_sum, running_out)


def local_general(
    span_queries,
    span_keys,
    span_values,
    cache_keys,
    cache_values,
    page_table,
    frame_lists,
    list_counts,
    out_weight,
):
    frames = lax.axis_size("fsdp")
    own_frame = lax.axis_index("fsdp")
    tokens_here = span_queries.shape[1]
    row_width = span_queries.shape[2]
    heads_here = row_width // HD
    max_slots = frame_lists.shape[1]
    own_queries = span_queries[0].reshape(tokens_here, heads_here, HD)
    own_keys = span_keys[0].reshape(tokens_here, heads_here, HD)
    own_values = span_values[0].reshape(tokens_here, heads_here, HD)
    destinations = jnp.arange(frames, dtype=jnp.int32)[:, None]
    blank = empty_state(tokens_here, heads_here)
    started = absorb(blank, own_queries, own_keys, own_values)
    slot_index = jnp.arange(max_slots, dtype=jnp.int32)[None, :]
    send_blocks = block_numbers(destinations, slot_index, page_table, frame_lists).T
    sent_keys, sent_values = pick_blocks(send_blocks, cache_keys, cache_values)
    arrived_keys, arrived_values = (
        lax.all_to_all(sent_keys, "fsdp", split_axis=1, concat_axis=1, tiled=True),
        lax.all_to_all(sent_values, "fsdp", split_axis=1, concat_axis=1, tiled=True),
    )
    arrived_keys = arrived_keys.reshape(max_slots, tokens_here, heads_here, HD)
    arrived_values = arrived_values.reshape(max_slots, tokens_here, heads_here, HD)
    item_count = lookup(list_counts, own_frame)

    def advance_own(item_number, carried_one):
        return absorb(
            carried_one, own_queries, arrived_keys[item_number], arrived_values[item_number]
        )

    final_state = lax.fori_loop(0, item_count, advance_own, started)
    running_sum = final_state[1]
    running_out = final_state[2]
    attended = (
        (running_out / running_sum[:, :, None]).astype(jnp.bfloat16).reshape(tokens_here, row_width)
    )
    partial_value = jnp.dot(
        attended,
        lax.all_gather(out_weight, "fsdp", axis=1, tiled=True),
        preferred_element_type=jnp.float32,
    )
    own_rows = lax.psum_scatter(
        partial_value.astype(jnp.bfloat16), "clip", scatter_dimension=0, tiled=True
    )
    return own_rows[None]


MESH = pl.DeviceIdType.MESH
LOG2E = 1.4426950408889634
VMEM_BYTES = 56 * 1024 * 1024


def attend_kernel(
    frames,
    slots,
    q_ref,
    k_ref,
    v_ref,
    ck_ref,
    cv_ref,
    page_ref,
    list_ref,
    count_ref,
    w_ref,
    out_ref,
    w_out,
    send,
    recv,
    qkv,
    stage,
    att_in,
    o_s,
    m_s,
    l_s,
    blk,
    send_sem,
    recv_sem,
    qkv_sem,
    att_sem,
    w_sem,
):
    me = lax.axis_index("fsdp")
    x_me = lax.rem(me, 2)
    partner = me + 1 - 2 * x_me
    heads = send.shape[0]
    half = heads * HD
    rows = q_ref.shape[0]
    scale = LOG2E / math.sqrt(HD)

    barrier = pltpu.get_barrier_semaphore()

    def greet(i, carry):
        pl.semaphore_signal(
            barrier, inc=1, device_id={"fsdp": lax.rem(me + i, frames)}, device_id_type=MESH
        )
        return carry

    lax.fori_loop(1, frames, greet, 0)
    pl.semaphore_wait(barrier, frames - 1)

    share = w_ref.shape[0]

    def flip(number, bits):
        for bit in (1, 2, 4, 8):
            if bits & bit:
                number = number + bit * (1 - 2 * lax.rem(number // bit, 2))
        return number

    def pass_on(away, hop):
        rows_at = pl.ds(pl.multiple_of(flip(me, away) * share, 16), share)
        return pltpu.make_async_remote_copy(
            src_ref=w_out.at[rows_at] if away else w_ref,
            dst_ref=w_out.at[rows_at],
            send_sem=w_sem.at[0, away ^ hop],
            recv_sem=w_sem.at[1, away ^ hop],
            device_id={"fsdp": flip(me, hop)},
            device_id_type=MESH,
        )

    passed = []

    def forward(aways, hops):
        for away in aways:
            if away:
                pass_on(away ^ 1, 1).wait_recv()
        for away in aways:
            for hop in hops:
                move = pass_on(away, hop)
                move.start()
                passed.append(move)

    own_share = pltpu.make_async_copy(
        w_ref, w_out.at[pl.ds(pl.multiple_of(me * share, 16), share)], w_sem.at[0, 0]
    )
    own_share.start()

    moves = []
    for t, ref in enumerate((q_ref, k_ref, v_ref)):
        theirs = pl.multiple_of((1 - x_me) * half, 128)
        mine = pl.multiple_of(x_me * half, 128)
        far = pltpu.make_async_remote_copy(
            src_ref=ref.at[:, pl.ds(theirs, half)],
            dst_ref=qkv.at[t, x_me],
            send_sem=qkv_sem.at[0, t],
            recv_sem=qkv_sem.at[1, t],
            device_id={"fsdp": partner},
            device_id_type=MESH,
        )
        near = pltpu.make_async_copy(
            ref.at[:, pl.ds(mine, half)], qkv.at[t, x_me], qkv_sem.at[2, t]
        )
        far.start()
        near.start()
        moves += [far, near]

    forward([0], [8, 4, 2, 1])

    def number(p, carry):
        first = count_ref[2 * p]
        for j in range(slots):
            late = jnp.where(j >= first, 1, 0)
            at = jnp.minimum(j - late * first, slots - 2)
            listed = list_ref[2 * p + late, at]
            blk[p * slots + j] = page_ref[(2 * p) // CF * NC + listed]
        return carry

    lax.fori_loop(0, frames // 2, number, 0)

    def transfer(h, there, slot):
        return pltpu.make_async_remote_copy(
            src_ref=send.at[h, there],
            dst_ref=recv.at[h, slot],
            send_sem=send_sem.at[h, there],
            recv_sem=recv_sem.at[h, slot],
            device_id={"fsdp": there},
            device_id_type=MESH,
        )

    for h in range(heads):

        def fill(i, carry):
            there = lax.rem(me + i, frames)
            col = pl.multiple_of(lax.rem(there, 2) * half + h * HD, 128)
            base = there // 2 * slots
            for j in range(slots):
                b = blk[base + j]
                send[h, there, 0, j] = ck_ref[b, :, pl.ds(col, HD)]
                send[h, there, 1, j] = cv_ref[b, :, pl.ds(col, HD)]
            transfer(h, there, me).start()
            return carry

        lax.fori_loop(1, frames, fill, 0)
        col = pl.multiple_of(x_me * half + h * HD, 128)
        for j in range(slots):
            b = blk[me // 2 * slots + j]
            recv[h, me, 0, j] = ck_ref[b, :, pl.ds(col, HD)]
            recv[h, me, 1, j] = cv_ref[b, :, pl.ds(col, HD)]
        if h == 1:
            forward([8], [4, 2, 1])
        if h == 2:
            forward([4, 12], [2, 1])

    for move in moves:
        move.wait()

    first_me = count_ref[me - x_me]

    def attend(j, q, k, v):
        s = lax.dot_general(
            q, k, (((1,), (1,)), ((), ())), preferred_element_type=jnp.float32
        )
        top = jnp.max(s, axis=1, keepdims=True)
        w = jnp.exp2((s - top) * scale)
        m_s[j] = top
        l_s[j] = jnp.sum(w, axis=1, keepdims=True)
        o_s[j] = jnp.dot(w.astype(jnp.bfloat16), v, preferred_element_type=jnp.float32)

    att_moves = []
    for h in range(heads):
        if h == 2:
            forward([1, 9, 5, 13], [2])
        cols = slice(h * HD, (h + 1) * HD)

        def own(f, carry):
            attend(slots + f, qkv[0, f, :, cols], qkv[1, f, :, cols], qkv[2, f, :, cols])
            return carry

        lax.fori_loop(0, 2, own, 0)

        def arrive(i, carry):
            there = lax.rem(me + i, frames)
            transfer(h, there, there).wait_recv()
            return carry

        lax.fori_loop(1, frames, arrive, 0)

        def listed(j, carry):
            f = jnp.where(j >= first_me, 1, 0)
            k = recv[h, :, 0, j].reshape(-1, HD)
            v = recv[h, :, 1, j].reshape(-1, HD)
            attend(j, qkv[0, f, :, cols], k, v)
            return carry

        lax.fori_loop(0, slots, listed, 0)

        for f in range(2):

            def live(j):
                if j >= slots:
                    return j - slots == f
                return (j < first_me) if f == 0 else (j >= first_me)

            tops = [
                m_s[j]
                if live(j) is True
                else jnp.where(live(j), m_s[j], jnp.float32(neg_fill))
                for j in range(slots + 2)
                if live(j) is not False
            ]
            top = functools.reduce(jnp.maximum, tops)
            total = jnp.zeros((rows, 1), jnp.float32)
            summed = jnp.zeros((rows, HD), jnp.float32)
            at = 0
            for j in range(slots + 2):
                if live(j) is False:
                    continue
                w = jnp.exp2((tops[at] - top) * scale)
                at += 1
                if live(j) is not True:
                    w = jnp.where(live(j), w, jnp.float32(0))
                total = total + w * l_s[j]
                summed = summed + w * o_s[j]
            stage[h, f] = (summed / total).astype(jnp.bfloat16)
        move = pltpu.make_async_remote_copy(
            src_ref=stage.at[h, 1 - x_me],
            dst_ref=att_in.at[h],
            send_sem=att_sem.at[0, h],
            recv_sem=att_sem.at[1, h],
            device_id={"fsdp": partner},
            device_id_type=MESH,
        )
        move.start()
        att_moves.append(move)
        out_ref[:, pl.ds(pl.multiple_of(x_me * half + h * HD, 128), HD)] = stage[h, x_me]

    for h in range(heads):
        att_moves[h].wait()
        out_ref[:, pl.ds(pl.multiple_of((1 - x_me) * half + h * HD, 128), HD)] = att_in[h]

    own_share.wait()
    for away in (2, 10, 6, 14, 3, 11, 7, 15):
        pass_on(away ^ 1, 1).wait_recv()
    for move in passed:
        move.wait_send()

    def drain(i, carry):
        there = lax.rem(me + i, frames)
        for h in range(heads):
            transfer(h, there, me).wait_send()
        return carry

    lax.fori_loop(1, frames, drain, 0)


def attend_pair(
    q, k, v, cache_keys, cache_values, page_table, frame_lists, list_counts, w_rows, frames
):
    rows, width = q.shape
    token_slice = cache_keys.shape[1]
    slots = frame_lists.shape[1] + 1
    heads = width // HD // 2
    block = (heads, frames, 2, slots, token_slice, HD)
    anywhere = pl.BlockSpec(memory_space=pl.ANY)
    vmem = pl.BlockSpec(memory_space=pltpu.VMEM)
    smem = pl.BlockSpec(memory_space=pltpu.SMEM)
    return pl.pallas_call(
        functools.partial(attend_kernel, frames, slots),
        out_shape=[
            jax.ShapeDtypeStruct((rows, width), jnp.bfloat16),
            jax.ShapeDtypeStruct((frames * w_rows.shape[0], w_rows.shape[1]), jnp.bfloat16),
        ],
        in_specs=[anywhere] * 3 + [vmem] * 2 + [smem] * 3 + [anywhere],
        out_specs=[vmem, anywhere],
        scratch_shapes=[
            pltpu.VMEM(block, jnp.bfloat16),
            pltpu.VMEM(block, jnp.bfloat16),
            pltpu.VMEM((3, 2, rows, heads * HD), jnp.bfloat16),
            pltpu.VMEM((heads, 2, rows, HD), jnp.bfloat16),
            pltpu.VMEM((heads, rows, HD), jnp.bfloat16),
            pltpu.VMEM((slots + 2, rows, HD), jnp.float32),
            pltpu.VMEM((slots + 2, rows, 1), jnp.float32),
            pltpu.VMEM((slots + 2, rows, 1), jnp.float32),
            pltpu.SMEM((frames // 2 * slots,), jnp.int32),
            pltpu.SemaphoreType.DMA((heads, frames)),
            pltpu.SemaphoreType.DMA((heads, frames)),
            pltpu.SemaphoreType.DMA((3, 3)),
            pltpu.SemaphoreType.DMA((2, heads)),
            pltpu.SemaphoreType.DMA((2, frames)),
        ],
        compiler_params=pltpu.CompilerParams(
            collective_id=0, has_side_effects=True, vmem_limit_bytes=VMEM_BYTES
        ),
        cost_estimate=pl.CostEstimate(
            flops=4 * rows * rows * HD * heads * (slots + 2),
            bytes_accessed=64 * 1024 * 1024,
            transcendentals=rows * rows * heads * (slots + 2),
        ),
    )(q, k, v, cache_keys, cache_values, page_table, frame_lists, list_counts, w_rows)


def project_kernel(att_ref, w_ref, out_ref, sent, came, kept, send_sem, recv_sem):
    step = pl.program_id(0)
    steps, rows, wide = sent.shape
    me = lax.axis_index("clip")
    sibling = 1 - me

    @pl.when(step == 0)
    def _():
        barrier = pltpu.get_barrier_semaphore()
        pl.semaphore_signal(barrier, inc=1, device_id={"clip": sibling}, device_id_type=MESH)
        pl.semaphore_wait(barrier, 1)

    def move(i):
        return pltpu.make_async_remote_copy(
            src_ref=sent.at[i],
            dst_ref=came.at[i],
            send_sem=send_sem.at[i],
            recv_sem=recv_sem.at[i],
            device_id={"clip": sibling},
            device_id_type=MESH,
        )

    def product(half):
        start = pl.multiple_of(half * rows, rows)
        return lax.dot_general(
            att_ref[pl.ds(start, rows), :],
            w_ref[...],
            (((1,), (1,)), ((), ())),
            preferred_element_type=jnp.float32,
        ).astype(jnp.bfloat16)

    sent[step] = product(sibling)
    move(step).start()
    kept[step] = product(me)

    @pl.when(step == steps - 1)
    def _():
        for i in range(steps):
            move(i).wait()
            out_ref[:, i * wide : (i + 1) * wide] = (
                kept[i].astype(jnp.float32) + came[i].astype(jnp.float32)
            ).astype(jnp.bfloat16)


def project(attended, weights):
    columns, depth = weights.shape
    steps = 4
    wide = columns // steps
    rows = attended.shape[0] // 2
    block = (steps, rows, wide)
    return pl.pallas_call(
        project_kernel,
        grid=(steps,),
        out_shape=jax.ShapeDtypeStruct((rows, columns), jnp.bfloat16),
        in_specs=[
            pl.BlockSpec((2 * rows, depth), lambda i: (0, 0)),
            pl.BlockSpec((wide, depth), lambda i: (i, 0)),
        ],
        out_specs=pl.BlockSpec((rows, columns), lambda i: (0, 0)),
        scratch_shapes=[
            pltpu.VMEM(block, jnp.bfloat16),
            pltpu.VMEM(block, jnp.bfloat16),
            pltpu.VMEM(block, jnp.bfloat16),
            pltpu.SemaphoreType.DMA((steps,)),
            pltpu.SemaphoreType.DMA((steps,)),
        ],
        compiler_params=pltpu.CompilerParams(
            collective_id=1, has_side_effects=True, vmem_limit_bytes=VMEM_BYTES
        ),
    )(attended, weights)


def local(
    span_queries,
    span_keys,
    span_values,
    cache_keys,
    cache_values,
    page_table,
    frame_lists,
    list_counts,
    out_weight,
):
    frames = lax.axis_size("fsdp")
    attended, weights = attend_pair(
        span_queries[0],
        span_keys[0],
        span_values[0],
        cache_keys,
        cache_values,
        page_table,
        frame_lists,
        list_counts,
        out_weight.T,
        frames,
    )
    return project(attended, weights)[None]


def solution(mesh):
    in_specs = (
        P("fsdp", None, "clip"),
        P("fsdp", None, "clip"),
        P("fsdp", None, "clip"),
        P(None, "fsdp", "clip"),
        P(None, "fsdp", "clip"),
        P(),
        P(),
        P(),
        P("clip", "fsdp"),
    )
    out_specs = P("fsdp", "clip", None)
    clip, fsdp = mesh.shape["clip"], mesh.shape["fsdp"]
    paired = clip == 2 and fsdp == 16
    body = local if paired else local_general
    return jax.shard_map(body, mesh=mesh, in_specs=in_specs, out_specs=out_specs, check_vma=False)
```

```python
import functools
import math

import jax
import jax.numpy as jnp
from jax import lax
from jax.experimental import pallas as pl
from jax.experimental.pallas import tpu as pltpu
from jax.sharding import PartitionSpec as P

HD = 128
CF = 8
NC = 16
FT = 512


neg_fill = -1e30


def lookup(values_table, positions):
    table_width = values_table.shape[0]
    matches = positions[..., None] == jnp.arange(table_width, dtype=jnp.int32)
    return jnp.sum(jnp.where(matches, values_table, 0), axis=-1)


def block_numbers(frame_index, slot_index, page_table, frame_lists):
    max_slots = frame_lists.shape[1]
    listed = lookup(frame_lists.reshape(-1), frame_index * max_slots + slot_index)
    return lookup(page_table, frame_index // CF * NC + listed)


def pick_blocks(send_blocks, cache_keys, cache_values):
    slot_total = send_blocks.shape[0]
    frames = send_blocks.shape[1]
    token_slice = cache_keys.shape[1]
    row_width = cache_keys.shape[2]
    sent_keys = cache_keys[send_blocks].reshape(slot_total, frames * token_slice, row_width)
    sent_values = cache_values[send_blocks].reshape(slot_total, frames * token_slice, row_width)
    return (sent_keys, sent_values)


def empty_state(tokens_here, heads_here):
    return (
        jnp.full((tokens_here, heads_here), neg_fill, jnp.float32),
        jnp.zeros((tokens_here, heads_here), jnp.float32),
        jnp.zeros((tokens_here, heads_here, HD), jnp.float32),
    )


def absorb(carried, query_block, key_block, value_block):
    running_max, running_sum, running_out = carried
    scores = jnp.einsum(
        "qhd,khd->qhk", query_block, key_block, preferred_element_type=jnp.float32
    ) * (1.0 / math.sqrt(HD))
    new_max = jnp.maximum(running_max, jnp.max(scores, axis=2))
    shrink = jnp.exp(running_max - new_max)
    weights = jnp.exp(scores - new_max[:, :, None])
    running_sum = running_sum * shrink + jnp.sum(weights, axis=2)
    running_out = running_out * shrink[:, :, None] + jnp.einsum(
        "qhk,khd->qhd",
        weights.astype(jnp.bfloat16),
        value_block,
        preferred_element_type=jnp.float32,
    )
    return (new_max, running_sum, running_out)


def local_general(
    span_queries,
    span_keys,
    span_values,
    cache_keys,
    cache_values,
    page_table,
    frame_lists,
    list_counts,
    out_weight,
):
    frames = lax.axis_size("fsdp")
    own_frame = lax.axis_index("fsdp")
    tokens_here = span_queries.shape[1]
    row_width = span_queries.shape[2]
    heads_here = row_width // HD
    max_slots = frame_lists.shape[1]
    own_queries = span_queries[0].reshape(tokens_here, heads_here, HD)
    own_keys = span_keys[0].reshape(tokens_here, heads_here, HD)
    own_values = span_values[0].reshape(tokens_here, heads_here, HD)
    destinations = jnp.arange(frames, dtype=jnp.int32)[:, None]
    blank = empty_state(tokens_here, heads_here)
    started = absorb(blank, own_queries, own_keys, own_values)
    slot_index = jnp.arange(max_slots, dtype=jnp.int32)[None, :]
    send_blocks = block_numbers(destinations, slot_index, page_table, frame_lists).T
    sent_keys, sent_values = pick_blocks(send_blocks, cache_keys, cache_values)
    arrived_keys, arrived_values = (
        lax.all_to_all(sent_keys, "fsdp", split_axis=1, concat_axis=1, tiled=True),
        lax.all_to_all(sent_values, "fsdp", split_axis=1, concat_axis=1, tiled=True),
    )
    arrived_keys = arrived_keys.reshape(max_slots, tokens_here, heads_here, HD)
    arrived_values = arrived_values.reshape(max_slots, tokens_here, heads_here, HD)
    item_count = lookup(list_counts, own_frame)

    def advance_own(item_number, carried_one):
        return absorb(
            carried_one, own_queries, arrived_keys[item_number], arrived_values[item_number]
        )

    final_state = lax.fori_loop(0, item_count, advance_own, started)
    running_sum = final_state[1]
    running_out = final_state[2]
    attended = (
        (running_out / running_sum[:, :, None]).astype(jnp.bfloat16).reshape(tokens_here, row_width)
    )
    partial_value = jnp.dot(
        attended,
        lax.all_gather(out_weight, "fsdp", axis=1, tiled=True),
        preferred_element_type=jnp.float32,
    )
    own_rows = lax.psum_scatter(
        partial_value.astype(jnp.bfloat16), "clip", scatter_dimension=0, tiled=True
    )
    return own_rows[None]


MESH = pl.DeviceIdType.MESH
LOG2E = 1.4426950408889634
VMEM_BYTES = 56 * 1024 * 1024


def attend_kernel(
    frames,
    slots,
    q_ref,
    k_ref,
    v_ref,
    ck_ref,
    cv_ref,
    page_ref,
    list_ref,
    count_ref,
    w_ref,
    out_ref,
    w_out,
    send,
    recv,
    qkv,
    stage,
    att_in,
    o_s,
    m_s,
    l_s,
    blk,
    send_sem,
    recv_sem,
    qkv_sem,
    att_sem,
    w_sem,
):
    me = lax.axis_index("fsdp")
    x_me = lax.rem(me, 2)
    partner = me + 1 - 2 * x_me
    heads = send.shape[0]
    half = heads * HD
    rows = q_ref.shape[0]
    scale = LOG2E / math.sqrt(HD)

    barrier = pltpu.get_barrier_semaphore()

    def greet(i, carry):
        pl.semaphore_signal(
            barrier, inc=1, device_id={"fsdp": lax.rem(me + i, frames)}, device_id_type=MESH
        )
        return carry

    lax.fori_loop(1, frames, greet, 0)
    pl.semaphore_wait(barrier, frames - 1)

    share = w_ref.shape[0]

    def flip(number, bits):
        for bit in (1, 2, 4, 8):
            if bits & bit:
                number = number + bit * (1 - 2 * lax.rem(number // bit, 2))
        return number

    def pass_on(away, hop):
        rows_at = pl.ds(pl.multiple_of(flip(me, away) * share, 16), share)
        return pltpu.make_async_remote_copy(
            src_ref=w_out.at[rows_at] if away else w_ref,
            dst_ref=w_out.at[rows_at],
            send_sem=w_sem.at[0, away ^ hop],
            recv_sem=w_sem.at[1, away ^ hop],
            device_id={"fsdp": flip(me, hop)},
            device_id_type=MESH,
        )

    passed = []

    def forward(aways, hops):
        for away in aways:
            if away:
                pass_on(away ^ 1, 1).wait_recv()
        for away in aways:
            for hop in hops:
                move = pass_on(away, hop)
                move.start()
                passed.append(move)

    own_share = pltpu.make_async_copy(
        w_ref, w_out.at[pl.ds(pl.multiple_of(me * share, 16), share)], w_sem.at[0, 0]
    )
    own_share.start()

    moves = []
    for t, ref in enumerate((q_ref, k_ref, v_ref)):
        theirs = pl.multiple_of((1 - x_me) * half, 128)
        mine = pl.multiple_of(x_me * half, 128)
        far = pltpu.make_async_remote_copy(
            src_ref=ref.at[:, pl.ds(theirs, half)],
            dst_ref=qkv.at[t, x_me],
            send_sem=qkv_sem.at[0, t],
            recv_sem=qkv_sem.at[1, t],
            device_id={"fsdp": partner},
            device_id_type=MESH,
        )
        near = pltpu.make_async_copy(
            ref.at[:, pl.ds(mine, half)], qkv.at[t, x_me], qkv_sem.at[2, t]
        )
        far.start()
        near.start()
        moves += [far, near]

    forward([0], [8, 4, 2, 1])

    def number(p, carry):
        first = count_ref[2 * p]
        for j in range(slots):
            late = jnp.where(j >= first, 1, 0)
            at = jnp.minimum(j - late * first, slots - 2)
            listed = list_ref[2 * p + late, at]
            blk[p * slots + j] = page_ref[(2 * p) // CF * NC + listed]
        return carry

    lax.fori_loop(0, frames // 2, number, 0)

    def transfer(h, there, slot):
        return pltpu.make_async_remote_copy(
            src_ref=send.at[h, there],
            dst_ref=recv.at[h, slot],
            send_sem=send_sem.at[h, there],
            recv_sem=recv_sem.at[h, slot],
            device_id={"fsdp": there},
            device_id_type=MESH,
        )

    for h in range(heads):

        def fill(i, carry):
            far = lax.rem(i, 2)
            step = far * (frames // 2) + i // 2
            there = lax.rem(me + step, frames)
            col = pl.multiple_of(lax.rem(there, 2) * half + h * HD, 128)
            base = there // 2 * slots
            for j in range(slots):
                b = blk[base + j]
                send[h, there, 0, j] = ck_ref[b, :, pl.ds(col, HD)]
                send[h, there, 1, j] = cv_ref[b, :, pl.ds(col, HD)]
            transfer(h, there, me).start()
            return carry

        lax.fori_loop(1, frames, fill, 0)
        col = pl.multiple_of(x_me * half + h * HD, 128)
        for j in range(slots):
            b = blk[me // 2 * slots + j]
            recv[h, me, 0, j] = ck_ref[b, :, pl.ds(col, HD)]
            recv[h, me, 1, j] = cv_ref[b, :, pl.ds(col, HD)]
        if h == 0:
            forward([8], [4, 2, 1])
        if h == 1:
            forward([4, 12], [2, 1])
        if h == 2:
            forward([1, 9, 5], [2])
            forward([14], [1])

    for move in moves:
        move.wait()

    first_me = count_ref[me - x_me]

    def attend(j, q, k, v):
        s = lax.dot_general(
            q, k, (((1,), (1,)), ((), ())), preferred_element_type=jnp.float32
        )
        top = jnp.max(s, axis=1, keepdims=True)
        w = jnp.exp2((s - top) * scale)
        m_s[j] = top
        l_s[j] = jnp.sum(w, axis=1, keepdims=True)
        o_s[j] = jnp.dot(w.astype(jnp.bfloat16), v, preferred_element_type=jnp.float32)

    att_moves = []
    for h in range(heads):
        cols = slice(h * HD, (h + 1) * HD)

        def own(f, carry):
            attend(slots + f, qkv[0, f, :, cols], qkv[1, f, :, cols], qkv[2, f, :, cols])
            return carry

        lax.fori_loop(0, 2, own, 0)

        def arrive(i, carry):
            there = lax.rem(me + i, frames)
            transfer(h, there, there).wait_recv()
            return carry

        lax.fori_loop(1, frames, arrive, 0)

        def listed(j, carry):
            f = jnp.where(j >= first_me, 1, 0)
            k = recv[h, :, 0, j].reshape(-1, HD)
            v = recv[h, :, 1, j].reshape(-1, HD)
            attend(j, qkv[0, f, :, cols], k, v)
            return carry

        lax.fori_loop(0, slots, listed, 0)

        for f in range(2):

            def live(j):
                if j >= slots:
                    return j - slots == f
                return (j < first_me) if f == 0 else (j >= first_me)

            tops = [
                m_s[j]
                if live(j) is True
                else jnp.where(live(j), m_s[j], jnp.float32(neg_fill))
                for j in range(slots + 2)
                if live(j) is not False
            ]
            top = functools.reduce(jnp.maximum, tops)
            total = jnp.zeros((rows, 1), jnp.float32)
            summed = jnp.zeros((rows, HD), jnp.float32)
            at = 0
            for j in range(slots + 2):
                if live(j) is False:
                    continue
                w = jnp.exp2((tops[at] - top) * scale)
                at += 1
                if live(j) is not True:
                    w = jnp.where(live(j), w, jnp.float32(0))
                total = total + w * l_s[j]
                summed = summed + w * o_s[j]
            stage[h, f] = (summed / total).astype(jnp.bfloat16)
        move = pltpu.make_async_remote_copy(
            src_ref=stage.at[h, 1 - x_me],
            dst_ref=att_in.at[h],
            send_sem=att_sem.at[0, h],
            recv_sem=att_sem.at[1, h],
            device_id={"fsdp": partner},
            device_id_type=MESH,
        )
        move.start()
        att_moves.append(move)
        out_ref[:, pl.ds(pl.multiple_of(x_me * half + h * HD, 128), HD)] = stage[h, x_me]

    for h in range(heads):
        att_moves[h].wait()
        out_ref[:, pl.ds(pl.multiple_of((1 - x_me) * half + h * HD, 128), HD)] = att_in[h]

    own_share.wait()
    for away in (2, 10, 6, 13, 3, 11, 7, 15):
        pass_on(away ^ 1, 1).wait_recv()
    for move in passed:
        move.wait_send()

    def drain(i, carry):
        there = lax.rem(me + i, frames)
        for h in range(heads):
            transfer(h, there, me).wait_send()
        return carry

    lax.fori_loop(1, frames, drain, 0)


def attend_pair(
    q, k, v, cache_keys, cache_values, page_table, frame_lists, list_counts, w_rows, frames
):
    rows, width = q.shape
    token_slice = cache_keys.shape[1]
    slots = frame_lists.shape[1] + 1
    heads = width // HD // 2
    block = (heads, frames, 2, slots, token_slice, HD)
    anywhere = pl.BlockSpec(memory_space=pl.ANY)
    vmem = pl.BlockSpec(memory_space=pltpu.VMEM)
    smem = pl.BlockSpec(memory_space=pltpu.SMEM)
    return pl.pallas_call(
        functools.partial(attend_kernel, frames, slots),
        out_shape=[
            jax.ShapeDtypeStruct((rows, width), jnp.bfloat16),
            jax.ShapeDtypeStruct((frames * w_rows.shape[0], w_rows.shape[1]), jnp.bfloat16),
        ],
        in_specs=[anywhere] * 3 + [vmem] * 2 + [smem] * 3 + [anywhere],
        out_specs=[vmem, anywhere],
        scratch_shapes=[
            pltpu.VMEM(block, jnp.bfloat16),
            pltpu.VMEM(block, jnp.bfloat16),
            pltpu.VMEM((3, 2, rows, heads * HD), jnp.bfloat16),
            pltpu.VMEM((heads, 2, rows, HD), jnp.bfloat16),
            pltpu.VMEM((heads, rows, HD), jnp.bfloat16),
            pltpu.VMEM((slots + 2, rows, HD), jnp.float32),
            pltpu.VMEM((slots + 2, rows, 1), jnp.float32),
            pltpu.VMEM((slots + 2, rows, 1), jnp.float32),
            pltpu.SMEM((frames // 2 * slots,), jnp.int32),
            pltpu.SemaphoreType.DMA((heads, frames)),
            pltpu.SemaphoreType.DMA((heads, frames)),
            pltpu.SemaphoreType.DMA((3, 3)),
            pltpu.SemaphoreType.DMA((2, heads)),
            pltpu.SemaphoreType.DMA((2, frames)),
        ],
        compiler_params=pltpu.CompilerParams(
            collective_id=0, has_side_effects=True, vmem_limit_bytes=VMEM_BYTES
        ),
        cost_estimate=pl.CostEstimate(
            flops=4 * rows * rows * HD * heads * (slots + 2),
            bytes_accessed=64 * 1024 * 1024,
            transcendentals=rows * rows * heads * (slots + 2),
        ),
    )(q, k, v, cache_keys, cache_values, page_table, frame_lists, list_counts, w_rows)


def project_kernel(att_ref, w_ref, out_ref, sent, came, kept, send_sem, recv_sem):
    step = pl.program_id(0)
    steps, rows, wide = sent.shape
    me = lax.axis_index("clip")
    sibling = 1 - me

    @pl.when(step == 0)
    def _():
        barrier = pltpu.get_barrier_semaphore()
        pl.semaphore_signal(barrier, inc=1, device_id={"clip": sibling}, device_id_type=MESH)
        pl.semaphore_wait(barrier, 1)

    def move(i):
        return pltpu.make_async_remote_copy(
            src_ref=sent.at[i],
            dst_ref=came.at[i],
            send_sem=send_sem.at[i],
            recv_sem=recv_sem.at[i],
            device_id={"clip": sibling},
            device_id_type=MESH,
        )

    def product(half):
        start = pl.multiple_of(half * rows, rows)
        return lax.dot_general(
            att_ref[pl.ds(start, rows), :],
            w_ref[...],
            (((1,), (1,)), ((), ())),
            preferred_element_type=jnp.float32,
        ).astype(jnp.bfloat16)

    sent[step] = product(sibling)
    move(step).start()
    kept[step] = product(me)

    @pl.when(step == steps - 1)
    def _():
        for i in range(steps):
            move(i).wait()
            out_ref[:, i * wide : (i + 1) * wide] = (
                kept[i].astype(jnp.float32) + came[i].astype(jnp.float32)
            ).astype(jnp.bfloat16)


def project(attended, weights):
    columns, depth = weights.shape
    steps = 4
    wide = columns // steps
    rows = attended.shape[0] // 2
    block = (steps, rows, wide)
    return pl.pallas_call(
        project_kernel,
        grid=(steps,),
        out_shape=jax.ShapeDtypeStruct((rows, columns), jnp.bfloat16),
        in_specs=[
            pl.BlockSpec((2 * rows, depth), lambda i: (0, 0)),
            pl.BlockSpec((wide, depth), lambda i: (i, 0)),
        ],
        out_specs=pl.BlockSpec((rows, columns), lambda i: (0, 0)),
        scratch_shapes=[
            pltpu.VMEM(block, jnp.bfloat16),
            pltpu.VMEM(block, jnp.bfloat16),
            pltpu.VMEM(block, jnp.bfloat16),
            pltpu.SemaphoreType.DMA((steps,)),
            pltpu.SemaphoreType.DMA((steps,)),
        ],
        compiler_params=pltpu.CompilerParams(
            collective_id=1, has_side_effects=True, vmem_limit_bytes=VMEM_BYTES
        ),
    )(attended, weights)


def local(
    span_queries,
    span_keys,
    span_values,
    cache_keys,
    cache_values,
    page_table,
    frame_lists,
    list_counts,
    out_weight,
):
    frames = lax.axis_size("fsdp")
    attended, weights = attend_pair(
        span_queries[0],
        span_keys[0],
        span_values[0],
        cache_keys,
        cache_values,
        page_table,
        frame_lists,
        list_counts,
        out_weight.T,
        frames,
    )
    return project(attended, weights)[None]


def solution(mesh):
    in_specs = (
        P("fsdp", None, "clip"),
        P("fsdp", None, "clip"),
        P("fsdp", None, "clip"),
        P(None, "fsdp", "clip"),
        P(None, "fsdp", "clip"),
        P(),
        P(),
        P(),
        P("clip", "fsdp"),
    )
    out_specs = P("fsdp", "clip", None)
    clip, fsdp = mesh.shape["clip"], mesh.shape["fsdp"]
    paired = clip == 2 and fsdp == 16
    body = local if paired else local_general
    return jax.shard_map(body, mesh=mesh, in_specs=in_specs, out_specs=out_specs, check_vma=False)
```
